32 devices in a mesh: seq: 4 (over x, core), dp: 8 (over z, y).
Axes of the slice: x: 2, y: 2, z: 4, core: 2. Of those that a mesh axis runs over, the one named last changes fastest.
Arguments:
- residual: bfloat16 [6144, 2560], P(('seq', 'dp')), may hold values from -6 to 6
- query_raw: bfloat16 [6144, 2560], P(('seq', 'dp')), may hold values from -60 to 60
- key_raw: bfloat16 [6144, 2560], P(('seq', 'dp')), may hold values from -60 to 60
- values: bfloat16 [6144, 2560], P(('seq', 'dp')), may hold values from -6 to 6
- residual_grad: bfloat16 [6144, 2560], P(('seq', 'dp')), may hold values from -6 to 6
- modulated_grad: bfloat16 [6144, 2560], P(('seq', 'dp')), may hold values from -6 to 6
- condition: float32 [8, 2, 2560], P('dp'), may hold values from -3 to 3
- modulation: float32 [2, 2560], P(None, ('seq', 'dp')), may hold values from -0.5 to 0.5
- norm_gains: float32 [2, 2560], P(None, ('seq', 'dp')), may hold values from 0.25 to 1.75
Outputs:
- input_grad: bfloat16 [6144, 2560], P(('seq', 'dp'))
- query_grad: bfloat16 [6144, 2560], P(('seq', 'dp'))
- key_grad: bfloat16 [6144, 2560], P(('seq', 'dp'))
- value_grad: bfloat16 [6144, 2560], P(('seq', 'dp'))
- param_grads: float32 [5, 2560], P(None, ('seq', 'dp'))
The draws below stay inside these ranges and needn't reach their ends.
All inputs are finite; a program needn't handle non-finite values.
Results may differ from the reference program's by a relative error of at most 0.009.
The reference program's roundings to bfloat16 on the way (of `normed_query`, `normed_key`, `weights_low`, `attended`, `attended_grad` and `score_grad`) count: a program that leaves them out, or rounds other values in their place, can miss the bound.
Values may be sent and summed in bfloat16 or wider, within the bound.
No kernel may reach another device: no remote copies, remote signals or barrier semaphores. Data moves between devices by JAX's collectives and lax.ppermute only.
A program may use at most 128 MiB of HBM per device.

```python
import jax
import jax.numpy as jnp
from jax import lax

HEAD_DIM = 128
D = 2560
TOK_DEV = 192
TOKENS = 768
CLIPS = 8
ROWS = 6144
N_SEQ = 4
N_DP = 8


def query_key_pair(key):
    base_key = jax.random.fold_in(key, 7)
    subkeys = jax.random.split(base_key, 3)
    query = jnp.clip(jax.random.normal(subkeys[1], (ROWS, D)), -6.0, 6.0)
    keyrows = jnp.clip(jax.random.normal(subkeys[2], (ROWS, D)), -6.0, 6.0)
    return (query, keyrows)


def draw_query_raw(key, part):
    return query_key_pair(key)[0].astype(jnp.bfloat16)


def draw_key_raw(key, part):
    return query_key_pair(key)[1].astype(jnp.bfloat16)


def strengthened(result, own_key, source, target, shards_of, factor):
    owner, partner = [(jnp.arange(result.shape[dim]) // (result.shape[dim] // shards_of)).reshape([-1 if axis == dim else 1 for axis in range(result.ndim)]) for dim in (source, target)]
    chosen = jax.random.permutation(own_key, shards_of)[partner]
    strong = (owner == chosen) | (owner == (partner + shards_of // 2) % shards_of)
    return jnp.where(strong, factor * result, result)


def level_of(key, dims, shards, low, high):
    level, own = 1.0, jax.random.fold_in(key, 6)
    for dim, blocks in shards:
        draws = jnp.exp(jax.random.uniform(jax.random.fold_in(own, dim), (blocks,), jnp.float32, low / len(shards), high / len(shards)))
        level = level * jnp.repeat(draws, dims[dim] // blocks).reshape([-1 if axis == dim else 1 for axis in range(len(dims))])
    return level


def bell_draw(own_key, shape, scale, bound, cuts=(), kind=jnp.bfloat16):
    gain = level_of(own_key, shape, cuts, -0.22, 0.18) if cuts else 1.0
    drawn = jax.random.normal(own_key, shape, jnp.float32) * scale * gain
    return jnp.minimum(jnp.maximum(drawn, -bound), bound).astype(kind)


def noise_with(own_key, shape, deviation, reach, cuts, heavy, held_as=jnp.bfloat16):
    result = deviation * jax.random.normal(own_key, shape, jnp.float32)
    if cuts:
        result = result * level_of(own_key, shape, cuts, -0.22, 0.18)
    return jnp.clip(strengthened(result, jax.random.fold_in(own_key, 3), *heavy), -reach, reach).astype(held_as)


def setup_inputs(seed: int = 0) -> dict:
    keys = jax.random.split(jax.random.key(seed), 10)
    return {
        "residual": bell_draw(keys[0], (ROWS, D), 1.0, 6.0, ((0, 32),)),
        "query_raw": draw_query_raw(jax.random.fold_in(keys[9], 71), 0),
        "key_raw": draw_key_raw(jax.random.fold_in(keys[9], 71), 0),
        "values": bell_draw(keys[3], (ROWS, D), 1.0, 6.0, ((0, 32),)),
        "residual_grad": bell_draw(keys[4], (ROWS, D), 1.0, 6.0, ((0, 32),)),
        "modulated_grad": noise_with(keys[5], (ROWS, D), 1.0, 6.0, ((0, 32),), (0, 1, 32, 2.75)),
        "condition": bell_draw(keys[6], (CLIPS, 2, D), 0.5, 3.0, ((0, 8),), jnp.float32),
        "modulation": jnp.clip(jax.random.uniform(keys[7], (2, D), jnp.float32, -0.5, 0.5) * level_of(keys[7], (2, D), ((1, 32),), -0.4, 0.0), -0.5, 0.5),
        "norm_gains": jnp.clip(1.0 + 0.15 * jax.random.normal(keys[8], (2, D), jnp.float32), 0.25, 1.75),
    }


epsilon = 1e-06

def split_heads(matrix, head_width):
    row_count = matrix.shape[0]
    return matrix.reshape(row_count, -1, head_width).transpose(1, 0, 2)

def merge_heads(stacked):
    return stacked.transpose(1, 0, 2).reshape(stacked.shape[1], -1)

def root_scale(raw_values):
    floats = raw_values.astype(jnp.float32)
    return lax.rsqrt(lax.optimization_barrier(jnp.mean(floats * floats, axis=1, keepdims=True)) + epsilon)

def head_scores(query_head, key_head):
    return lax.dot_general(query_head, key_head, (((1,), (1,)), ((), ())), preferred_element_type=jnp.float32) * query_head.shape[-1] ** (-0.5)

def head_forward(pieces):
    query_head, key_head, value_head = pieces
    scores = head_scores(query_head, key_head)
    row_max = lax.optimization_barrier(jnp.max(scores, axis=1, keepdims=True))
    row_sum = lax.optimization_barrier(jnp.sum(jnp.exp(scores - row_max), axis=1, keepdims=True))
    logsum = row_max + jnp.log(row_sum)
    weights_low = jnp.exp(scores - logsum).astype(jnp.bfloat16)
    attended = jnp.dot(weights_low, value_head, preferred_element_type=jnp.float32).astype(jnp.bfloat16)
    return (attended, logsum[:, 0])

def head_backward(pieces):
    query_head, key_head, value_head, attended, attended_grad, logsum = pieces
    scores = head_scores(query_head, key_head)
    weights = jnp.exp(scores - logsum[:, None])
    row_dot = lax.optimization_barrier(jnp.sum(attended_grad.astype(jnp.float32) * attended.astype(jnp.float32), axis=1, keepdims=True))
    weight_grad = lax.dot_general(attended_grad, value_head, (((1,), (1,)), ((), ())), preferred_element_type=jnp.float32)
    score_grad = (weights * (weight_grad - row_dot) * query_head.shape[-1] ** (-0.5)).astype(jnp.bfloat16)
    value_part = lax.dot_general(weights.astype(jnp.bfloat16), attended_grad, (((0,), (0,)), ((), ())), preferred_element_type=jnp.float32)
    query_part = jnp.dot(score_grad, key_head, preferred_element_type=jnp.float32)
    key_part = lax.dot_general(score_grad, query_head, (((0,), (0,)), ((), ())), preferred_element_type=jnp.float32)
    return (query_part, key_part, value_part)

def stream_pass(residual, attended, modulated, residual_grad, modulated_grad):
    gate_row = modulated[0]
    scale_row = modulated[1]
    summed = residual.astype(jnp.float32) + gate_row * attended.astype(jnp.float32)
    centered = summed - lax.optimization_barrier(jnp.mean(summed, axis=1, keepdims=True))
    norm_scale = lax.rsqrt(lax.optimization_barrier(jnp.mean(centered * centered, axis=1, keepdims=True)) + epsilon)
    normed = centered * norm_scale
    scaled_grad = modulated_grad.astype(jnp.float32) * (1.0 + scale_row)
    stream_grad = residual_grad.astype(jnp.float32) + norm_scale * (scaled_grad - lax.optimization_barrier(jnp.mean(scaled_grad, axis=1, keepdims=True)) - normed * lax.optimization_barrier(jnp.mean(scaled_grad * normed, axis=1, keepdims=True)))
    attended_grad = (stream_grad * gate_row).astype(jnp.bfloat16)
    return (stream_grad, normed, attended_grad)

def norm_backward(raw_values, inverse, gain_row, upstream):
    floats = raw_values.astype(jnp.float32)
    weighted = gain_row * upstream
    return (inverse * weighted - floats * inverse ** 3 * lax.optimization_barrier(jnp.mean(floats * weighted, axis=1, keepdims=True))).astype(jnp.bfloat16)

def partial_sums(attended, stream_grad, normed, modulated_grad, query_raw, query_scale, query_part, key_raw, key_scale, key_part):
    grad_floats = modulated_grad.astype(jnp.float32)
    return jnp.stack([lax.optimization_barrier(jnp.sum(stream_grad * attended.astype(jnp.float32), axis=0)), lax.optimization_barrier(jnp.sum(grad_floats, axis=0)), lax.optimization_barrier(jnp.sum(grad_floats * normed, axis=0)), lax.optimization_barrier(jnp.sum(query_part * query_raw.astype(jnp.float32) * query_scale, axis=0)), lax.optimization_barrier(jnp.sum(key_part * key_raw.astype(jnp.float32) * key_scale, axis=0))])

def reference(residual, query_raw, key_raw, values, residual_grad, modulated_grad, condition, modulation, norm_gains):

    def clip_major(matrix):
        return matrix.reshape(N_SEQ, N_DP, TOK_DEV, D).transpose(1, 0, 2, 3).reshape(N_DP, TOKENS, D)

    def row_major(matrix):
        return matrix.reshape(N_DP, N_SEQ, TOK_DEV, D).transpose(1, 0, 2, 3).reshape(ROWS, D)

    def clip_pass(pieces):
        clip_resid, clip_query, clip_key, clip_values, clip_rgrad, clip_mgrad, clip_cond = pieces
        modulated = modulation + clip_cond
        query_scale = root_scale(clip_query)
        key_scale = root_scale(clip_key)
        normed_query = (clip_query.astype(jnp.float32) * query_scale * norm_gains[0]).astype(jnp.bfloat16)
        normed_key = (clip_key.astype(jnp.float32) * key_scale * norm_gains[1]).astype(jnp.bfloat16)
        query_heads = split_heads(normed_query, HEAD_DIM)
        key_heads = split_heads(normed_key, HEAD_DIM)
        value_heads = split_heads(clip_values, HEAD_DIM)
        attended_heads, logsum = lax.map(head_forward, (query_heads, key_heads, value_heads))
        attended = merge_heads(attended_heads)
        stream_grad, normed, attended_grad = stream_pass(clip_resid, attended, modulated, clip_rgrad, clip_mgrad)
        query_part, key_part, value_part = lax.map(head_backward, (query_heads, key_heads, value_heads, attended_heads, split_heads(attended_grad, HEAD_DIM), logsum))
        query_part = merge_heads(query_part)
        key_part = merge_heads(key_part)
        value_part = merge_heads(value_part)
        sums_here = partial_sums(attended, stream_grad, normed, clip_mgrad, clip_query, query_scale, query_part, clip_key, key_scale, key_part)
        return (stream_grad.astype(jnp.bfloat16), norm_backward(clip_query, query_scale, norm_gains[0], query_part), norm_backward(clip_key, key_scale, norm_gains[1], key_part), value_part.astype(jnp.bfloat16), sums_here)
    results = lax.map(clip_pass, (clip_major(residual), clip_major(query_raw), clip_major(key_raw), clip_major(values), clip_major(residual_grad), clip_major(modulated_grad), condition))
    return (row_major(results[0]), row_major(results[1]), row_major(results[2]), row_major(results[3]), lax.optimization_barrier(jnp.sum(results[4], axis=0)) * ROWS ** (-0.5))
```

```python
import functools

import jax
import jax.numpy as jnp
from jax import lax
from jax.experimental import pallas as pl
from jax.experimental.pallas import tpu as pltpu
from jax.sharding import PartitionSpec as P

HEAD = 128
EPS = 1e-06
CHUNKS = 2
STRIP = 16
VMEM_LIMIT = 56 * 1024 * 1024

ANY = pl.BlockSpec(memory_space=pl.ANY)
VMEM = pl.BlockSpec(memory_space=pltpu.VMEM)
SOFT = HEAD ** (-0.5)


def nt_dot(left, right):
    return lax.dot_general(left, right, (((1,), (1,)), ((), ())), preferred_element_type=jnp.float32)


def nn_dot(left, right):
    return jnp.dot(left, right, preferred_element_type=jnp.float32)


def start_copies(pairs, sems, first=0):
    copies = [
        pltpu.make_async_copy(source, target, sems.at[first + index])
        for index, (source, target) in enumerate(pairs)
    ]
    for copy in copies:
        copy.start()
    return copies


def wait_all(copies):
    for copy in copies:
        copy.wait()


def strips(count, body):
    def step(index, carry):
        body(pl.multiple_of(index * STRIP, STRIP))
        return carry

    lax.fori_loop(0, count // STRIP, step, 0)


def root_scale(floats):
    return lax.rsqrt(jnp.mean(floats * floats, axis=1, keepdims=True) + EPS)


def fold8(matrix):
    return matrix[:8] + matrix[8:]


def norm_kernel(raw_ref, gain_ref, out_ref):
    gain = gain_ref[0:1, :]

    def body(row):
        floats = raw_ref[pl.ds(row, STRIP), :].astype(jnp.float32)
        out_ref[pl.ds(row, STRIP), :] = (floats * root_scale(floats) * gain).astype(jnp.bfloat16)

    strips(raw_ref.shape[0], body)


def forward_kernel(chunks, *refs):
    (qn_in, k0, k1, k2, k3, v0, v1, v2, v3, res_in, rgrad_in, mgrad_in, gains, modulated) = refs[:14]
    (ig_out, do_out, kn_out, lse_out, rd_out, stats_out, sums_out) = refs[14:21]
    send_outs = refs[21 : 21 + chunks]
    (qn, keys, vals, res, rgrad, mgrad, att, ig, dout, lse_s, rd_s, acc, sems) = refs[21 + chunks :]
    rows, width = qn.shape
    heads = width // HEAD
    key_copies = start_copies(
        [(ref, keys.at[pl.ds(i * rows, rows)]) for i, ref in enumerate((k0, k1, k2, k3))], sems, 0
    )
    q_copy = start_copies([(qn_in, qn)], sems, 4)
    val_copies = start_copies(
        [(ref, vals.at[pl.ds(i * rows, rows)]) for i, ref in enumerate((v0, v1, v2, v3))], sems, 5
    )
    row_copies = start_copies([(res_in, res), (rgrad_in, rgrad), (mgrad_in, mgrad)], sems, 9)
    wait_all(key_copies)
    gain = gains[1:2, :]

    def norm_body(row):
        floats = keys[pl.ds(row, STRIP), :].astype(jnp.float32)
        keys[pl.ds(row, STRIP), :] = (floats * root_scale(floats) * gain).astype(jnp.bfloat16)

    strips(4 * rows, norm_body)
    kn_copy = start_copies([(keys, kn_out)], sems, 12)
    wait_all(q_copy)
    wait_all(val_copies)
    lse_s[...] = jnp.zeros_like(lse_s)
    rd_s[...] = jnp.zeros_like(rd_s)
    lane = lax.broadcasted_iota(jnp.int32, (rows, HEAD), 1)

    def head_body(pair, carry):
        for part in range(2):
            head = pair * 2 + part
            cols = pl.ds(pl.multiple_of(head * HEAD, HEAD), HEAD)
            scores = nt_dot(qn[:, cols], keys[:, cols]) * SOFT
            row_max = jnp.max(scores, axis=1, keepdims=True)
            weights = jnp.exp(scores - row_max)
            row_sum = jnp.sum(weights, axis=1, keepdims=True)
            weights_low = (weights * (1.0 / row_sum)).astype(jnp.bfloat16)
            att[:, cols] = nn_dot(weights_low, vals[:, cols]).astype(jnp.bfloat16)
            logsum = row_max + jnp.log(row_sum)
            lse_s[pl.ds(0, rows), :] = jnp.where(lane == head, logsum, lse_s[pl.ds(0, rows), :])
        return carry

    lax.fori_loop(0, heads // 2, head_body, 0)
    wait_all(row_copies)
    acc[...] = jnp.zeros_like(acc)
    gate = modulated[0:1, :]
    scale1 = 1.0 + modulated[1:2, :]
    lane16 = lax.broadcasted_iota(jnp.int32, (STRIP, HEAD), 1)

    def stream_body(row):
        here = pl.ds(row, STRIP)
        attended = att[here, :].astype(jnp.float32)
        summed = res[here, :].astype(jnp.float32) + gate * attended
        centered = summed - jnp.mean(summed, axis=1, keepdims=True)
        norm_scale = lax.rsqrt(jnp.mean(centered * centered, axis=1, keepdims=True) + EPS)
        normed = centered * norm_scale
        mg = mgrad[here, :].astype(jnp.float32)
        scaled = mg * scale1
        stream = rgrad[here, :].astype(jnp.float32) + norm_scale * (
            scaled
            - jnp.mean(scaled, axis=1, keepdims=True)
            - normed * jnp.mean(scaled * normed, axis=1, keepdims=True)
        )
        ig[here, :] = stream.astype(jnp.bfloat16)
        grad_low = (stream * gate).astype(jnp.bfloat16)
        dout[here, :] = grad_low
        acc[0:8, :] += fold8(stream * attended)
        acc[8:16, :] += fold8(mg)
        acc[16:24, :] += fold8(mg * normed)
        product = grad_low.astype(jnp.float32) * attended
        dots = jnp.zeros((STRIP, HEAD), jnp.float32)
        for head in range(heads):
            one = jnp.sum(product[:, head * HEAD : (head + 1) * HEAD], axis=1, keepdims=True)
            dots = jnp.where(lane16 == head, one, dots)
        rd_s[here, :] = dots

    strips(rows, stream_body)
    part = width // chunks
    outs = [(dout.at[:, pl.ds(i * part, part)], ref) for i, ref in enumerate(send_outs)]
    out_copies = start_copies(outs + [(dout, do_out), (ig, ig_out)], sems, 13)
    lse_out[...] = lse_s[pl.ds(0, rows), :]
    rd_out[...] = rd_s[pl.ds(0, rows), :]
    half = stats_out.shape[0] // 2
    stats_out[0:half, :] = lse_s[...].T[:half, :rows]
    stats_out[half:, :] = rd_s[...].T[:half, :rows]
    sums_out[...] = jnp.concatenate(
        [jnp.sum(acc[i * 8 : i * 8 + 8, :], axis=0, keepdims=True) for i in range(3)], axis=0
    )
    wait_all(kn_copy)
    wait_all(out_copies)


def query_kernel(*refs):
    (qn_in, kn_in, v0, v1, v2, v3, do_in, raw_in, lse, rd, gains) = refs[:11]
    (grad_out, sums_out) = refs[11:13]
    (qn, keys, vals, dout, raw, dqn, dots, grad, sems) = refs[13:]
    rows, width = qn.shape
    heads = width // HEAD
    copies = start_copies(
        [(kn_in, keys), (qn_in, qn), (do_in, dout)]
        + [(ref, vals.at[pl.ds(i * rows, rows)]) for i, ref in enumerate((v0, v1, v2, v3))]
        + [(raw_in, raw)],
        sems,
        0,
    )
    wait_all(copies)
    lane = lax.broadcasted_iota(jnp.int32, (rows, HEAD), 1)

    def head_body(pair, carry):
        for part in range(2):
            head = pair * 2 + part
            cols = pl.ds(pl.multiple_of(head * HEAD, HEAD), HEAD)
            chosen = lane == head
            logsum = jnp.sum(jnp.where(chosen, lse[...], 0.0), axis=1, keepdims=True)
            row_dot = jnp.sum(jnp.where(chosen, rd[...], 0.0), axis=1, keepdims=True)
            weights = jnp.exp(nt_dot(qn[:, cols], keys[:, cols]) * SOFT - logsum)
            weight_grad = nt_dot(dout[:, cols], vals[:, cols])
            score_grad = (weights * (weight_grad - row_dot) * SOFT).astype(jnp.bfloat16)
            dqn[:, cols] = nn_dot(score_grad, keys[:, cols])
        return carry

    lax.fori_loop(0, heads // 2, head_body, 0)
    dots[...] = jnp.zeros_like(dots)
    gain_q = gains[0:1, :]

    def final_body(row):
        here = pl.ds(row, STRIP)
        floats = raw[here, :].astype(jnp.float32)
        inverse = root_scale(floats)
        upstream = dqn[here, :]
        weighted = gain_q * upstream
        grad[here, :] = (
            inverse * weighted
            - floats * (inverse * inverse * inverse) * jnp.mean(floats * weighted, axis=1, keepdims=True)
        ).astype(jnp.bfloat16)
        dots[0:8, :] += fold8(upstream * floats * inverse)
        dots[8:16, :] += fold8(upstream * qn[here, :].astype(jnp.float32))

    strips(rows, final_body)
    out_copy = start_copies([(grad, grad_out)], sems, 8)
    sums_out[0:1, :] = jnp.sum(dots[0:8, :], axis=0, keepdims=True)
    sums_out[1:2, :] = jnp.sum(dots[8:16, :], axis=0, keepdims=True) / gains[1:2, :]
    wait_all(out_copy)


def key_heads(first, heads, keys, vals, queries, douts, stats, emit):
    half = stats.shape[0] // 2

    def one(head):
        cols = pl.ds(pl.multiple_of(head * HEAD, HEAD), HEAD)
        logsum = stats[pl.ds(head + first, 1), :]
        row_dot = stats[pl.ds(head + first + half, 1), :]
        weights = jnp.exp(nt_dot(keys[:, cols], queries[:, cols]) * SOFT - logsum)
        weight_grad = nt_dot(vals[:, cols], douts[:, cols])
        score_grad = (weights * (weight_grad - row_dot) * SOFT).astype(jnp.bfloat16)
        emit(
            cols,
            nn_dot(score_grad, queries[:, cols]),
            nn_dot(weights.astype(jnp.bfloat16), douts[:, cols]),
        )

    def body(index, carry):
        one(index * 2)
        one(index * 2 + 1)
        return carry

    lax.fori_loop(0, heads // 2, body, 0)


def key_local_kernel(*refs):
    (kn_in, v_in, qa, qb, da, db, stats, acck_out, accv_out) = refs[:9]
    (keys, vals, queries, douts, sems) = refs[9:]
    rows, width = keys.shape
    copies = start_copies(
        [
            (kn_in.at[pl.ds(0, rows)], keys),
            (v_in, vals),
            (qa, queries.at[pl.ds(0, rows)]),
            (qb, queries.at[pl.ds(rows, rows)]),
            (da, douts.at[pl.ds(0, rows)]),
            (db, douts.at[pl.ds(rows, rows)]),
        ],
        sems,
    )
    wait_all(copies)

    def emit(cols, key_part, value_part):
        acck_out[:, cols] = key_part
        accv_out[:, cols] = value_part

    key_heads(0, width // HEAD, keys, vals, queries, douts, stats, emit)


def key_remote_kernel(index, chunks, *refs):
    final = index == chunks - 1
    (kn_in, v_in, qa, qb, da, db, stats, acck_in, accv_in) = refs[:9]
    refs = refs[9:]
    if final:
        raw_in, gains = refs[:2]
        early_k = refs[2 : 1 + chunks]
        early_v = refs[1 + chunks : 2 * chunks]
        (kgrad_out, vgrad_out) = refs[2 * chunks : 2 * chunks + 2]
        (keys, vals, queries, douts, sems, raw, upstream, vgrad, kgrad) = refs[2 * chunks + 2 :]
    else:
        (dk_out, dv_out) = refs[:2]
        (keys, vals, queries, douts, sems, acck, accv) = refs[2:]
    rows, width = keys.shape
    base = index * width
    span = pl.ds(base, width)
    pairs = [
        (kn_in.at[pl.ds(0, rows), span], keys),
        (v_in.at[:, span], vals),
        (qa.at[:, span], queries.at[pl.ds(0, rows)]),
        (qb.at[:, span], queries.at[pl.ds(rows, rows)]),
        (da, douts.at[pl.ds(0, rows)]),
        (db, douts.at[pl.ds(rows, rows)]),
    ]
    if final:
        pairs += [(acck_in.at[:, span], upstream.at[:, span])]
        pairs += [(ref, upstream.at[:, pl.ds(i * width, width)]) for i, ref in enumerate(early_k)]
        pairs += [(ref, vgrad.at[:, pl.ds(i * width, width)]) for i, ref in enumerate(early_v)]
        pairs += [(raw_in, raw)]
    else:
        pairs += [(acck_in.at[:, span], acck), (accv_in.at[:, span], accv)]
    wait_all(start_copies(pairs, sems))

    def emit(cols, key_part, value_part):
        if final:
            place = pl.ds(pl.multiple_of(cols.start + base, HEAD), HEAD)
            upstream[:, place] += key_part
            vgrad[:, place] = (accv_in[:, cols] + value_part).astype(jnp.bfloat16)
        else:
            dk_out[:, cols] = acck[:, cols] + key_part
            dv_out[:, cols] = (accv[:, cols] + value_part).astype(jnp.bfloat16)

    key_heads(base // HEAD, width // HEAD, keys, vals, queries, douts, stats, emit)
    if final:
        v_copy = start_copies([(vgrad, vgrad_out)], sems, 0)
        gain = gains[1:2, :]

        def final_body(row):
            here = pl.ds(row, STRIP)
            floats = raw[here, :].astype(jnp.float32)
            inverse = root_scale(floats)
            weighted = gain * upstream[here, :]
            kgrad[here, :] = (
                inverse * weighted
                - floats
                * (inverse * inverse * inverse)
                * jnp.mean(floats * weighted, axis=1, keepdims=True)
            ).astype(jnp.bfloat16)

        strips(rows, final_body)
        wait_all(start_copies([(kgrad, kgrad_out)], sems, 1))
        wait_all(v_copy)


def params(flops=0, moved=0):
    return dict(
        compiler_params=pltpu.CompilerParams(vmem_limit_bytes=VMEM_LIMIT),
        cost_estimate=pl.CostEstimate(flops=flops, bytes_accessed=moved, transcendentals=0),
    )


def bf(*shape):
    return jax.ShapeDtypeStruct(shape, jnp.bfloat16)


def fl(*shape):
    return jax.ShapeDtypeStruct(shape, jnp.float32)


def vb(*shape):
    return pltpu.VMEM(shape, jnp.bfloat16)


def vf(*shape):
    return pltpu.VMEM(shape, jnp.float32)


def per_device(
    residual,
    query_raw,
    key_raw,
    values,
    residual_grad,
    modulated_grad,
    condition,
    modulation,
    norm_gains,
):
    rows, width = residual.shape
    seq = lax.axis_size("seq")
    devices = seq * lax.axis_size("dp")
    chunks = CHUNKS
    heads = width // HEAD
    half = -(-heads // 8) * 8
    unit = 2 * rows * rows * width
    across = functools.partial(lax.ppermute, axis_name="seq", perm=[(i, i ^ 2) for i in range(seq)])
    beside = functools.partial(lax.ppermute, axis_name="seq", perm=[(i, i ^ 1) for i in range(seq)])

    key_x = across(key_raw)
    value_x = across(values)
    key_s = beside(key_raw)
    value_s = beside(values)
    rows_here = jnp.concatenate([modulation, norm_gains], axis=0)
    rows_all = lax.all_gather(rows_here, ("seq", "dp"), axis=0, tiled=False)
    rows_all = rows_all.transpose(1, 0, 2).reshape(4, width)
    modulated = rows_all[:2] + condition[0]
    gains = rows_all[2:]

    normed_query = pl.pallas_call(
        norm_kernel,
        out_shape=bf(rows, width),
        in_specs=[VMEM, VMEM],
        out_specs=VMEM,
        name="norm_query",
        **params(0, 4 * rows * width),
    )(query_raw, gains)
    query_s = beside(normed_query)
    query_x = across(normed_query)
    key_d = beside(key_x)
    value_d = beside(value_x)

    part = width // chunks
    outs = pl.pallas_call(
        functools.partial(forward_kernel, chunks),
        out_shape=(
            bf(rows, width),
            bf(rows, width),
            bf(4 * rows, width),
            fl(rows, HEAD),
            fl(rows, HEAD),
            fl(2 * half, rows),
            fl(3, width),
        )
        + (bf(rows, part),) * chunks,
        in_specs=[ANY] * 12 + [VMEM] * 2,
        out_specs=(ANY, ANY, ANY, VMEM, VMEM, VMEM, VMEM) + (ANY,) * chunks,
        scratch_shapes=[
            vb(rows, width),
            vb(4 * rows, width),
            vb(4 * rows, width),
            vb(rows, width),
            vb(rows, width),
            vb(rows, width),
            vb(rows, width),
            vb(rows, width),
            vb(rows, width),
            vf(2 * HEAD, HEAD),
            vf(2 * HEAD, HEAD),
            vf(24, width),
            pltpu.SemaphoreType.DMA((15 + chunks,)),
        ],
        name="forward",
        **params(8 * unit, 40 * rows * width),
    )(
        normed_query,
        key_raw,
        key_s,
        key_x,
        key_d,
        values,
        value_s,
        value_x,
        value_d,
        residual,
        residual_grad,
        modulated_grad,
        gains,
        modulated,
    )
    input_grad, dout, normed_keys, lse, row_dot, stats, sums3 = outs[:7]
    sends = outs[7:]
    stats_x = across(stats)
    dout_x = [across(one) for one in sends]
    dout_s = beside(dout)
    stats_s = beside(stats)
    query_d = beside(query_x)
    stats_d = beside(stats_x)
    dout_d = [beside(one) for one in dout_x]

    query_grad, sums2 = pl.pallas_call(
        query_kernel,
        out_shape=(bf(rows, width), fl(2, width)),
        in_specs=[ANY] * 8 + [VMEM] * 3,
        out_specs=(ANY, VMEM),
        scratch_shapes=[
            vb(rows, width),
            vb(4 * rows, width),
            vb(4 * rows, width),
            vb(rows, width),
            vb(rows, width),
            vf(rows, width),
            vf(16, width),
            vb(rows, width),
            pltpu.SemaphoreType.DMA((9,)),
        ],
        name="query_side",
        **params(12 * unit, 30 * rows * width),
    )(
        normed_query,
        normed_keys,
        values,
        value_s,
        value_x,
        value_d,
        dout,
        query_raw,
        lse,
        row_dot,
        gains,
    )
    sums = jnp.concatenate([sums3, sums2], axis=0)
    sums = sums.reshape(5, devices, width // devices).transpose(1, 0, 2)
    moved = lax.all_to_all(sums, ("seq", "dp"), split_axis=0, concat_axis=0, tiled=True)
    factor = (rows * devices) ** (-0.5)
    param_grads = jnp.sum(moved, axis=0) * factor

    acck, accv = pl.pallas_call(
        key_local_kernel,
        out_shape=(fl(rows, width), fl(rows, width)),
        in_specs=[ANY] * 6 + [VMEM],
        out_specs=(VMEM, VMEM),
        scratch_shapes=[
            vb(rows, width),
            vb(rows, width),
            vb(2 * rows, width),
            vb(2 * rows, width),
            pltpu.SemaphoreType.DMA((6,)),
        ],
        name="key_side_local",
        **params(8 * unit, 24 * rows * width),
    )(
        normed_keys,
        values,
        normed_query,
        query_s,
        dout,
        dout_s,
        jnp.concatenate([stats, stats_s], axis=1),
    )
    stats_far = jnp.concatenate([stats_x, stats_d], axis=1)
    early = []
    for index in range(chunks):
        final = index == chunks - 1
        operands = [
            normed_keys,
            values,
            query_x,
            query_d,
            dout_x[index],
            dout_d[index],
            stats_far,
            acck,
            accv[:, index * part :] if final else accv,
        ]
        specs = [ANY] * 6 + [VMEM] + [ANY, VMEM if final else ANY]
        scratch = [
            vb(rows, part),
            vb(rows, part),
            vb(2 * rows, part),
            vb(2 * rows, part),
            pltpu.SemaphoreType.DMA((8 + 2 * chunks,)),
        ]
        if final:
            operands += [key_raw, gains] + [one[0] for one in early] + [one[1] for one in early]
            specs += [ANY, VMEM] + [ANY] * (2 * len(early))
            shapes = (bf(rows, width), bf(rows, width))
            out_specs = (ANY, ANY)
            scratch += [vb(rows, width), vf(rows, width), vb(rows, width), vb(rows, width)]
        else:
            shapes = (fl(rows, part), bf(rows, part))
            out_specs = (VMEM, VMEM)
            scratch += [vf(rows, part), vf(rows, part)]
        done = pl.pallas_call(
            functools.partial(key_remote_kernel, index, chunks),
            out_shape=shapes,
            in_specs=specs,
            out_specs=out_specs,
            scratch_shapes=scratch,
            name="key_side_far_last" if final else "key_side_far",
            **params(8 * unit // chunks, 24 * rows * part),
        )(*operands)
        early.append(done)
    key_grad, value_grad = early[-1]
    return (input_grad, query_grad, key_grad, value_grad, param_grads)


def solution(mesh):
    placed = (P(("seq", "dp"), None),) * 6 + (
        P("dp", None, None),
        P(None, ("seq", "dp")),
        P(None, ("seq", "dp")),
    )
    return jax.shard_map(
        per_device,
        mesh=mesh,
        in_specs=placed,
        out_specs=(P(("seq", "dp"), None),) * 4 + (P(None, ("seq", "dp")),),
        check_vma=False,
    )
```

```python
import functools

import jax
import jax.numpy as jnp
from jax import lax
from jax.experimental import pallas as pl
from jax.experimental.pallas import tpu as pltpu
from jax.sharding import PartitionSpec as P

HEAD = 128
EPS = 1e-06
GROUP = 4
STRIP = 16
MIB = 1024 * 1024

ANY = pl.BlockSpec(memory_space=pl.ANY)
VMEM = pl.BlockSpec(memory_space=pltpu.VMEM)
SOFT = HEAD ** (-0.5)


def nt_dot(left, right):
    return lax.dot_general(left, right, (((1,), (1,)), ((), ())), preferred_element_type=jnp.float32)


def nn_dot(left, right):
    return jnp.dot(left, right, preferred_element_type=jnp.float32)


class Loads:
    def __init__(self, pairs, sems, groups):
        self.pairs, self.sems, self.groups = pairs, sems, groups
        self.step = pairs[0][1].shape[1] // groups

    def at(self, index, group):
        source, target = self.pairs[index]
        cols = pl.ds(pl.multiple_of(group * self.step, HEAD), self.step)
        return pltpu.make_async_copy(source.at[:, cols], target.at[:, cols], self.sems.at[index, group])

    def start(self):
        for group in range(self.groups):
            for index in range(len(self.pairs)):
                self.at(index, group).start()

    def wait(self, group):
        for index in range(len(self.pairs)):
            self.at(index, group).wait()


def start_copies(pairs, sems, first=0):
    copies = [
        pltpu.make_async_copy(source, target, sems.at[first + index])
        for index, (source, target) in enumerate(pairs)
    ]
    for copy in copies:
        copy.start()
    return copies


def wait_all(copies):
    for copy in copies:
        copy.wait()


def strips(count, unroll, body):
    def step(index, carry):
        base = index * (STRIP * unroll)
        body([pl.ds(pl.multiple_of(base + i * STRIP, STRIP), STRIP) for i in range(unroll)])
        return carry

    lax.fori_loop(0, count // (STRIP * unroll), step, 0)


def root_scale(floats):
    return lax.rsqrt(jnp.mean(floats * floats, axis=1, keepdims=True) + EPS)


def fold8(matrix):
    return matrix[:8] + matrix[8:]


def norm_kernel(query_in, key_in, gains, qn_out, qsend_out, kn_out):
    def one(source, target, gain, copy):
        def body(spans):
            floats = [source[span, :].astype(jnp.float32) for span in spans]
            scales = [root_scale(each) for each in floats]
            for span, scale in zip(spans, scales):
                low = (source[span, :].astype(jnp.float32) * scale * gain).astype(jnp.bfloat16)
                target[span, :] = low
                if copy is not None:
                    copy[span, :] = low

        strips(source.shape[0], 4, body)

    one(key_in, kn_out, gains[1:2, :], None)
    one(query_in, qn_out, gains[0:1, :], qsend_out)


def hold_kernel(held, before, out):
    del held, before, out


def forward_kernel(sends, *refs):
    (qn_in, k0, k1, k2, k3, v0, v1, v2, v3, res_in, rgrad_in, mgrad_in, modulated) = refs[:13]
    (ig_out, do_out, lse_out, rd_out, stats_out, sums_out, send_out) = refs[13:20]
    (qn, keys, vals, res, rgrad, mgrad, att, ig, dout, lse_s, rd_s, acc, sems, row_sems) = refs[20:]
    rows, width = qn.shape
    heads = width // HEAD
    groups = heads // GROUP
    loads = Loads(
        [(qn_in, qn)]
        + [(ref, keys.at[pl.ds(i * rows, rows)]) for i, ref in enumerate((k0, k1, k2, k3))]
        + [(ref, vals.at[pl.ds(i * rows, rows)]) for i, ref in enumerate((v0, v1, v2, v3))],
        sems,
        groups,
    )
    loads.start()
    row_copies = start_copies([(res_in, res), (rgrad_in, rgrad), (mgrad_in, mgrad)], row_sems, 0)
    lse_s[...] = jnp.zeros_like(lse_s)
    rd_s[...] = jnp.zeros_like(rd_s)
    acc[...] = jnp.zeros_like(acc)
    lane = lax.broadcasted_iota(jnp.int32, (rows, HEAD), 1)

    def head_body(group, carry):
        loads.wait(group)
        cols = [
            pl.ds(pl.multiple_of((group * GROUP + i) * HEAD, HEAD), HEAD) for i in range(GROUP)
        ]
        scores = [nt_dot(qn[:, col], keys[:, col]) for col in cols]
        tops = [jnp.max(score, axis=1, keepdims=True) for score in scores]
        weights = [jnp.exp((score - top) * SOFT) for score, top in zip(scores, tops)]
        totals = [jnp.sum(weight, axis=1, keepdims=True) for weight in weights]
        lows = [
            (weight * (1.0 / total)).astype(jnp.bfloat16) for weight, total in zip(weights, totals)
        ]
        results = [nn_dot(low, vals[:, col]).astype(jnp.bfloat16) for low, col in zip(lows, cols)]
        logs = lse_s[pl.ds(0, rows), :]
        for i in range(GROUP):
            att[:, cols[i]] = results[i]
            logs = jnp.where(lane == group * GROUP + i, tops[i] * SOFT + jnp.log(totals[i]), logs)
        lse_s[pl.ds(0, rows), :] = logs
        return carry

    lax.fori_loop(0, groups, head_body, 0)
    wait_all(row_copies)
    gate = modulated[0:1, :]
    scale1 = 1.0 + modulated[1:2, :]
    owner = lax.broadcasted_iota(jnp.int32, (width, HEAD), 0) // HEAD
    member = (owner == lax.broadcasted_iota(jnp.int32, (width, HEAD), 1)).astype(jnp.bfloat16)

    def stream_body(spans):
        def mean(matrix):
            return jnp.sum(matrix, axis=1, keepdims=True) * (1.0 / width)

        centers, scaled_means = [], []
        for span in spans:
            summed = res[span, :].astype(jnp.float32) + gate * att[span, :].astype(jnp.float32)
            centers.append(mean(summed))
            scaled_means.append(mean(mgrad[span, :].astype(jnp.float32) * scale1))
        norm_scales, dots = [], []
        for span, center in zip(spans, centers):
            summed = res[span, :].astype(jnp.float32) + gate * att[span, :].astype(jnp.float32)
            centered = summed - center
            norm_scales.append(lax.rsqrt(mean(centered * centered) + EPS))
            dots.append(mean(mgrad[span, :].astype(jnp.float32) * scale1 * centered))
        for span, center, scaled_mean, norm_scale, dot in zip(
            spans, centers, scaled_means, norm_scales, dots
        ):
            attended = att[span, :].astype(jnp.float32)
            normed = (res[span, :].astype(jnp.float32) + gate * attended - center) * norm_scale
            mg = mgrad[span, :].astype(jnp.float32)
            stream = rgrad[span, :].astype(jnp.float32) + norm_scale * (
                mg * scale1 - scaled_mean - normed * (dot * norm_scale)
            )
            ig[span, :] = stream.astype(jnp.bfloat16)
            grad_low = (stream * gate).astype(jnp.bfloat16)
            dout[span, :] = grad_low
            acc[0:8, :] += fold8(stream * attended)
            acc[8:16, :] += fold8(mg)
            acc[16:24, :] += fold8(mg * normed)
            product = grad_low.astype(jnp.float32) * attended
            high = product.astype(jnp.bfloat16)
            low = (product - high.astype(jnp.float32)).astype(jnp.bfloat16)
            rd_s[span, :] = nn_dot(high, member) + nn_dot(low, member)

    strips(rows, 2, stream_body)
    out_copies = start_copies(
        [(dout.at[:, pl.ds(0, sends)], send_out), (dout, do_out), (ig, ig_out)], row_sems, 0
    )
    lse_out[...] = lse_s[pl.ds(0, rows), :]
    rd_out[...] = rd_s[pl.ds(0, rows), :]
    half = stats_out.shape[0] // 2
    stats_out[0:half, :] = lse_s[...].T[:half, :rows]
    stats_out[half:, :] = rd_s[...].T[:half, :rows]
    sums_out[...] = jnp.concatenate(
        [jnp.sum(acc[i * 8 : i * 8 + 8, :], axis=0, keepdims=True) for i in range(3)], axis=0
    )
    wait_all(out_copies)


def query_kernel(sends, *refs):
    (qn_in, k0, k1, k2, k3, v0, v1, v2, v3, do_in, raw_in, lse, rd, gains) = refs[:14]
    (grad_out, sums_out, send_out) = refs[14:17]
    (qn, keys, vals, dout, raw, dqn, dots, grad, sems, row_sems) = refs[17:]
    rows, width = qn.shape
    heads = width // HEAD
    groups = heads // GROUP
    send = start_copies([(do_in.at[:, pl.ds(sends, width - sends)], send_out)], row_sems, 0)
    loads = Loads(
        [(qn_in, qn), (do_in, dout)]
        + [(ref, keys.at[pl.ds(i * rows, rows)]) for i, ref in enumerate((k0, k1, k2, k3))]
        + [(ref, vals.at[pl.ds(i * rows, rows)]) for i, ref in enumerate((v0, v1, v2, v3))],
        sems,
        groups,
    )
    loads.start()
    raw_copy = start_copies([(raw_in, raw)], row_sems, 1)

    def head_body(group, carry):
        loads.wait(group)
        cols = [
            pl.ds(pl.multiple_of((group * GROUP + i) * HEAD, HEAD), HEAD) for i in range(GROUP)
        ]
        shift = HEAD - group * GROUP
        logs = pltpu.roll(lse[...], shift, 1)
        row_dots = pltpu.roll(rd[...], shift, 1)
        weights = [
            jnp.exp(nt_dot(qn[:, col], keys[:, col]) * SOFT - logs[:, i : i + 1])
            for i, col in enumerate(cols)
        ]
        weight_grads = [nt_dot(dout[:, col], vals[:, col]) for col in cols]
        score_grads = [
            (weight * (weight_grad - row_dots[:, i : i + 1]) * SOFT).astype(jnp.bfloat16)
            for i, (weight, weight_grad) in enumerate(zip(weights, weight_grads))
        ]
        results = [nn_dot(score_grad, keys[:, col]) for score_grad, col in zip(score_grads, cols)]
        for col, result in zip(cols, results):
            dqn[:, col] = result
        return carry

    lax.fori_loop(0, groups, head_body, 0)
    wait_all(raw_copy)
    dots[...] = jnp.zeros_like(dots)
    gain_q = gains[0:1, :]

    def final_body(spans):
        floats = [raw[span, :].astype(jnp.float32) for span in spans]
        inverses = [root_scale(each) for each in floats]
        means = [
            jnp.mean(raw[span, :].astype(jnp.float32) * gain_q * dqn[span, :], axis=1, keepdims=True)
            for span in spans
        ]
        for span, inverse, mean in zip(spans, inverses, means):
            each = raw[span, :].astype(jnp.float32)
            upstream = dqn[span, :]
            grad[span, :] = (
                inverse * (gain_q * upstream) - each * (inverse * inverse * inverse * mean)
            ).astype(jnp.bfloat16)
            dots[0:8, :] += fold8(upstream * each * inverse)
            dots[8:16, :] += fold8(upstream * qn[span, :].astype(jnp.float32))

    strips(rows, 4, final_body)
    out_copy = start_copies([(grad, grad_out)], row_sems, 2)
    sums_out[0:1, :] = jnp.sum(dots[0:8, :], axis=0, keepdims=True)
    sums_out[1:2, :] = jnp.sum(dots[8:16, :], axis=0, keepdims=True) / gains[1:2, :]
    wait_all(send)
    wait_all(out_copy)


def key_heads(first, step, group, keys, vals, queries, douts, stats, emit):
    half = stats.shape[0] // 2
    heads = [group * step + i for i in range(step)]
    cols = [pl.ds(pl.multiple_of(head * HEAD, HEAD), HEAD) for head in heads]
    weights = [
        jnp.exp(
            nt_dot(keys[:, col], queries[:, col]) * SOFT - stats[pl.ds(head + first, 1), :]
        )
        for head, col in zip(heads, cols)
    ]
    weight_grads = [nt_dot(vals[:, col], douts[:, col]) for col in cols]
    value_parts = [
        nn_dot(weight.astype(jnp.bfloat16), douts[:, col]) for weight, col in zip(weights, cols)
    ]
    score_grads = [
        (
            weight * (weight_grad - stats[pl.ds(head + first + half, 1), :]) * SOFT
        ).astype(jnp.bfloat16)
        for weight, weight_grad, head in zip(weights, weight_grads, heads)
    ]
    key_parts = [nn_dot(grad, queries[:, col]) for grad, col in zip(score_grads, cols)]
    for col, key_part, value_part in zip(cols, key_parts, value_parts):
        emit(col, key_part, value_part)


def key_local_kernel(*refs):
    (kn_in, v_in, qa, qb, da, db, stats, acck_out, accv_out) = refs[:9]
    (keys, vals, queries, douts, sems) = refs[9:]
    rows, width = keys.shape
    groups = width // HEAD // GROUP
    loads = Loads(
        [
            (kn_in, keys),
            (v_in, vals),
            (qa, queries.at[pl.ds(0, rows)]),
            (qb, queries.at[pl.ds(rows, rows)]),
            (da, douts.at[pl.ds(0, rows)]),
            (db, douts.at[pl.ds(rows, rows)]),
        ],
        sems,
        groups,
    )
    loads.start()

    def emit(cols, key_part, value_part):
        acck_out[:, cols] = key_part
        accv_out[:, cols] = value_part

    def body(group, carry):
        loads.wait(group)
        key_heads(0, GROUP, group, keys, vals, queries, douts, stats, emit)
        return carry

    lax.fori_loop(0, groups, body, 0)


def key_far_kernel(base, final, *refs):
    (kn_in, v_in, qa, qb, da, db, stats, acck_in, accv_in) = refs[:9]
    refs = refs[9:]
    if final:
        (raw_in, gains, early_k, early_v, kgrad_out, vgrad_out) = refs[:6]
        (keys, vals, queries, douts, sems, row_sems, acck, accv, raw, upstream, vgrad, kgrad) = refs[6:]
    else:
        (dk_out, dv_out) = refs[:2]
        (keys, vals, queries, douts, sems, row_sems, acck, accv) = refs[2:]
    rows, width = keys.shape
    step = 5
    groups = width // HEAD // step
    span = pl.ds(base, width)
    loads = Loads(
        [
            (kn_in.at[:, span], keys),
            (v_in.at[:, span], vals),
            (qa.at[:, span], queries.at[pl.ds(0, rows)]),
            (qb.at[:, span], queries.at[pl.ds(rows, rows)]),
            (da, douts.at[pl.ds(0, rows)]),
            (db, douts.at[pl.ds(rows, rows)]),
            (acck_in.at[:, span], acck),
            (accv_in.at[:, span], accv),
        ],
        sems,
        groups,
    )
    loads.start()
    if final:
        before = pl.ds(0, base)
        row_copies = start_copies(
            [
                (early_k, upstream.at[:, before]),
                (early_v, vgrad.at[:, before]),
                (raw_in, raw),
            ],
            row_sems,
            0,
        )

    def emit(cols, key_part, value_part):
        if final:
            place = pl.ds(pl.multiple_of(cols.start + base, HEAD), HEAD)
            upstream[:, place] = acck[:, cols] + key_part
            vgrad[:, place] = (accv[:, cols] + value_part).astype(jnp.bfloat16)
        else:
            dk_out[:, cols] = acck[:, cols] + key_part
            dv_out[:, cols] = (accv[:, cols] + value_part).astype(jnp.bfloat16)

    for group in range(groups):
        loads.wait(group)
        key_heads(base // HEAD, step, group, keys, vals, queries, douts, stats, emit)
    if final:
        wait_all(row_copies)
        v_copy = start_copies([(vgrad, vgrad_out)], row_sems, 0)
        gain = gains[1:2, :]

        def final_body(spans):
            inverses = [root_scale(raw[each, :].astype(jnp.float32)) for each in spans]
            means = [
                jnp.mean(
                    raw[each, :].astype(jnp.float32) * gain * upstream[each, :],
                    axis=1,
                    keepdims=True,
                )
                for each in spans
            ]
            for each, inverse, mean in zip(spans, inverses, means):
                kgrad[each, :] = (
                    inverse * (gain * upstream[each, :])
                    - raw[each, :].astype(jnp.float32) * (inverse * inverse * inverse * mean)
                ).astype(jnp.bfloat16)

        strips(rows, 4, final_body)
        wait_all(start_copies([(kgrad, kgrad_out)], row_sems, 1))
        wait_all(v_copy)


def params(limit, flops, moved):
    return dict(
        compiler_params=pltpu.CompilerParams(vmem_limit_bytes=limit * MIB),
        cost_estimate=pl.CostEstimate(flops=flops, bytes_accessed=moved, transcendentals=0),
    )


def bf(*shape):
    return jax.ShapeDtypeStruct(shape, jnp.bfloat16)


def fl(*shape):
    return jax.ShapeDtypeStruct(shape, jnp.float32)


def vb(*shape):
    return pltpu.VMEM(shape, jnp.bfloat16)


def vf(*shape):
    return pltpu.VMEM(shape, jnp.float32)


def dma(*shape):
    return pltpu.SemaphoreType.DMA(shape)


def hold(held, before):
    return pl.pallas_call(
        hold_kernel,
        out_shape=jax.ShapeDtypeStruct(held.shape, held.dtype),
        in_specs=[ANY, ANY],
        out_specs=ANY,
        input_output_aliases={0: 0},
        name="hold",
        **params(1, 0, 0),
    )(held, before)


def per_device(
    residual,
    query_raw,
    key_raw,
    values,
    residual_grad,
    modulated_grad,
    condition,
    modulation,
    norm_gains,
):
    rows, width = residual.shape
    seq = lax.axis_size("seq")
    clips = lax.axis_size("dp")
    devices = seq * clips
    heads = width // HEAD
    groups = heads // GROUP
    half = -(-heads // 8) * 8
    unit = 2 * rows * (4 * rows) * width
    here = lax.axis_index("seq")
    across = functools.partial(lax.ppermute, axis_name="seq", perm=[(i, i ^ 2) for i in range(seq)])
    beside = functools.partial(lax.ppermute, axis_name="seq", perm=[(i, i ^ 1) for i in range(seq)])

    small = jnp.concatenate([modulation, norm_gains], axis=0)[None]
    other = beside(small)
    pair = jnp.where(
        here & 1 == 0, jnp.concatenate([small, other], 0), jnp.concatenate([other, small], 0)
    )
    other = across(pair)
    quad = jnp.where(
        here >> 1 == 0, jnp.concatenate([pair, other], 0), jnp.concatenate([other, pair], 0)
    )
    value_x = across(values)
    value_s = beside(values)
    rows_all = lax.all_gather(quad.reshape(1, -1), "dp", axis=0, tiled=True)
    rows_all = rows_all.reshape(clips, seq, 4, width // devices).transpose(2, 1, 0, 3).reshape(4, width)
    modulated = rows_all[:2] + condition[0]
    gains = rows_all[2:]

    normed_query, query_send, normed_key = pl.pallas_call(
        norm_kernel,
        out_shape=(bf(rows, width),) * 3,
        in_specs=[VMEM] * 3,
        out_specs=(VMEM,) * 3,
        name="norm_query_key",
        **params(16, 0, 10 * rows * width),
    )(query_raw, key_raw, gains)
    key_x = across(normed_key)
    key_s = beside(normed_key)
    query_s = beside(normed_query)
    value_d = beside(value_x)
    key_d = beside(key_x)
    query_send = hold(query_send, key_x)
    query_x = across(query_send)

    first = width // 2
    second = width - first
    input_grad, dout, lse, row_dot, stats, sums3, send_a = pl.pallas_call(
        functools.partial(forward_kernel, first),
        out_shape=(
            bf(rows, width),
            bf(rows, width),
            fl(rows, HEAD),
            fl(rows, HEAD),
            fl(2 * half, rows),
            fl(3, width),
            bf(rows, first),
        ),
        in_specs=[ANY] * 12 + [VMEM],
        out_specs=(ANY, ANY, VMEM, VMEM, VMEM, VMEM, ANY),
        scratch_shapes=[
            vb(rows, width),
            vb(4 * rows, width),
            vb(4 * rows, width),
            vb(rows, width),
            vb(rows, width),
            vb(rows, width),
            vb(rows, width),
            vb(rows, width),
            vb(rows, width),
            vf(2 * HEAD, HEAD),
            vf(2 * HEAD, HEAD),
            vf(24, width),
            dma(9, groups),
            dma(3),
        ],
        name="forward",
        **params(32, 4 * unit, 34 * rows * width),
    )(
        normed_query,
        normed_key,
        key_s,
        key_x,
        key_d,
        values,
        value_s,
        value_x,
        value_d,
        residual,
        residual_grad,
        modulated_grad,
        modulated,
    )
    stats_x = across(stats)
    dout_xa = across(send_a)
    dout_s = beside(dout)
    stats_s = beside(stats)
    query_d = beside(query_x)
    stats_d = beside(stats_x)

    query_grad, sums2, send_b = pl.pallas_call(
        functools.partial(query_kernel, first),
        out_shape=(bf(rows, width), fl(2, width), bf(rows, second)),
        in_specs=[ANY] * 11 + [VMEM] * 3,
        out_specs=(ANY, VMEM, ANY),
        scratch_shapes=[
            vb(rows, width),
            vb(4 * rows, width),
            vb(4 * rows, width),
            vb(rows, width),
            vb(rows, width),
            vf(rows, width),
            vf(16, width),
            vb(rows, width),
            dma(10, groups),
            dma(3),
        ],
        name="query_side",
        **params(32, 6 * unit, 30 * rows * width),
    )(
        normed_query,
        normed_key,
        key_s,
        key_x,
        key_d,
        values,
        value_s,
        value_x,
        value_d,
        dout,
        query_raw,
        lse,
        row_dot,
        gains,
    )
    dout_xb = across(send_b)
    dout_da = beside(dout_xa)
    sums = jnp.concatenate([sums3, sums2], axis=0)
    sums = sums.reshape(5, seq, clips, -1).transpose(2, 0, 1, 3).reshape(clips, -1)
    moved = lax.all_to_all(sums, "dp", split_axis=0, concat_axis=0, tiled=True)
    moved = jnp.sum(moved, axis=0).reshape(5, seq, -1).transpose(1, 0, 2).reshape(seq, -1)

    acck, accv = pl.pallas_call(
        key_local_kernel,
        out_shape=(fl(rows, width), fl(rows, width)),
        in_specs=[ANY] * 6 + [VMEM],
        out_specs=(VMEM, VMEM),
        scratch_shapes=[
            vb(rows, width),
            vb(rows, width),
            vb(2 * rows, width),
            vb(2 * rows, width),
            dma(6, groups),
        ],
        name="key_side_local",
        **params(32, 4 * unit, 24 * rows * width),
    )(
        normed_key,
        values,
        normed_query,
        query_s,
        dout,
        dout_s,
        jnp.concatenate([stats, stats_s], axis=1),
    )
    dout_xb = hold(dout_xb, acck)
    dout_db = beside(dout_xb)
    stats_far = jnp.concatenate([stats_x, stats_d], axis=1)

    def far(base, part, dout_x, dout_d, *early):
        operands = [normed_key, values, query_x, query_d, dout_x, dout_d, stats_far, acck, accv]
        specs = [ANY] * 6 + [VMEM, ANY, ANY]
        scratch = [
            vb(rows, part),
            vb(rows, part),
            vb(2 * rows, part),
            vb(2 * rows, part),
            dma(8, part // HEAD // 5),
            dma(3),
            vf(rows, part),
            vf(rows, part),
        ]
        if early:
            operands += [key_raw, gains, *early]
            specs += [ANY, VMEM, ANY, ANY]
            shapes = (bf(rows, width), bf(rows, width))
            out_specs = (ANY, ANY)
            scratch += [vb(rows, width), vf(rows, width), vb(rows, width), vb(rows, width)]
        else:
            shapes = (fl(rows, part), bf(rows, part))
            out_specs = (VMEM, VMEM)
        return pl.pallas_call(
            functools.partial(key_far_kernel, base, bool(early)),
            out_shape=shapes,
            in_specs=specs,
            out_specs=out_specs,
            scratch_shapes=scratch,
            name="key_side_far_last" if early else "key_side_far",
            **params(24, 4 * unit * part // width, 24 * rows * part),
        )(*operands)

    early = far(0, first, dout_xa, dout_da)
    moved = lax.all_to_all(hold(moved, early[0]), "seq", split_axis=0, concat_axis=0, tiled=True)
    factor = (rows * devices) ** (-0.5)
    param_grads = jnp.sum(moved, axis=0).reshape(5, -1) * factor
    key_grad, value_grad = far(first, second, dout_xb, dout_db, *early)
    return (input_grad, query_grad, key_grad, value_grad, param_grads)


def solution(mesh):
    placed = (P(("seq", "dp"), None),) * 6 + (
        P("dp", None, None),
        P(None, ("seq", "dp")),
        P(None, ("seq", "dp")),
    )
    return jax.shard_map(
        per_device,
        mesh=mesh,
        in_specs=placed,
        out_specs=(P(("seq", "dp"), None),) * 4 + (P(None, ("seq", "dp")),),
        check_vma=False,
    )
```
